256 devices in a mesh: ints: 16 (over x, y), amp: 16 (over z, core).
Axes of the slice: x: 4, y: 4, z: 8, core: 2. Of those that a mesh axis runs over, the one named last changes fastest.
Arguments:
- amplitudes: bfloat16 [1024, 32768], P('amp', 'ints'), may hold values from -6 to 6
- integrals: bfloat16 [32768, 16384], P('ints', 'amp'), may hold values from -0.125 to 0.125
- tile_map: int32 [16, 128], replicated, may hold values from 0 to 255, as said below
- residual_in: float32 [1024, 32768], P('amp', 'ints'), may hold values from -6 to 6
Outputs:
- residual: float32 [1024, 32768], P('amp', 'ints')
The draws below stay inside these ranges and needn't reach their ends.
Inputs may be any that keep to these rules, and one draw needn't show every extreme that they name: `tile_map`: each row i names 128 different tiles, exactly 128 // 16 of them from each run of 16 consecutive tiles (t // 16 equal).
All inputs are finite; a program needn't handle non-finite values.
Results may differ from the reference program's by a relative error of at most 0.0003.
Values may be sent and summed in bfloat16 or wider, within the bound.
A program may use at most 64 MiB of HBM per device.

```python
import jax
import jax.numpy as jnp

TILE = 128
TPD = 16
ABD = 8
OPS = 1024
NVP = 32768
SLOTS = 128
N_INTS = 16
N_AMP = 16


def draw_tile_map(key, part):
    key = jax.random.fold_in(key, 7)
    per_owner = N_AMP * ABD // N_INTS

    def one_block(block_key):
        return jax.random.permutation(block_key, TPD)[:per_owner]

    def one_row(row_key):
        subkeys = jax.random.split(row_key, N_INTS + 1)
        chosen = jax.vmap(one_block)(subkeys[:N_INTS])
        chosen = chosen + (jnp.arange(N_INTS, dtype=jnp.int32) * TPD)[:, None]
        return jax.random.permutation(subkeys[N_INTS], chosen.reshape(-1))
    return jax.vmap(one_row)(jax.random.split(key, N_INTS)).astype(jnp.int32)


def shard_levels(rng, shape, cuts, low, high):
    factor_of, own = 1.0, jax.random.fold_in(rng, 6)
    for position, parts in cuts:
        heights = jnp.exp(jax.random.uniform(jax.random.fold_in(own, position), (parts,), jnp.float32, low / len(cuts), high / len(cuts)))
        factor_of = factor_of * jnp.repeat(heights, shape[position] // parts).reshape([-1 if axis == position else 1 for axis in range(len(shape))])
    return factor_of


def bell_draw(stream_key, extent, scale, limit, cuts=(), held_as=jnp.bfloat16):
    factor_of = shard_levels(stream_key, extent, cuts, -0.22, 0.18) if cuts else 1.0
    drawn = jax.random.normal(stream_key, extent, jnp.float32) * scale * factor_of
    return jnp.minimum(jnp.maximum(drawn, -limit), limit).astype(held_as)


def setup_inputs(seed: int = 0) -> dict:
    seeds = jax.random.split(jax.random.key(seed), 5)
    return {
        "amplitudes": bell_draw(seeds[0], (OPS, NVP), 1.0, 6.0, ((0, 16), (1, 16))),
        "integrals": bell_draw(seeds[1], (NVP, SLOTS * TILE), (TPD * TILE) ** -0.5, 0.125, ((0, 16), (1, 16))),
        "tile_map": draw_tile_map(jax.random.fold_in(seeds[4], 71), 0),
        "residual_in": bell_draw(seeds[3], (OPS, NVP), 1.0, 6.0, ((0, 16), (1, 16)), jnp.float32),
    }


def reference(amplitudes, integrals, tile_map, residual_in):
    col_span = TPD * TILE
    ladder = jnp.zeros((OPS, N_INTS * TPD, TILE), jnp.float32)
    for owner_block in range(N_INTS):
        columns = amplitudes[:, owner_block * col_span:(owner_block + 1) * col_span]
        weights = integrals[owner_block * col_span:(owner_block + 1) * col_span]
        partial_value = jnp.dot(columns, weights, preferred_element_type=jnp.float32)
        partial_value = partial_value.reshape(OPS, N_AMP * ABD, TILE)
        ladder = ladder.at[:, tile_map[owner_block]].add(partial_value)
    return residual_in + ladder.reshape(OPS, N_INTS * TPD * TILE)
```

```python
import math

import jax
import jax.numpy as jnp
from jax import lax
from jax.experimental import pallas as pl
from jax.experimental.pallas import tpu as pltpu
from jax.sharding import PartitionSpec as P

MESH = pl.DeviceIdType.MESH
F32, BF16, I16 = jnp.float32, jnp.bfloat16, jnp.int16

TOP = math.log2(1537.0)
SPAN = 24.0
STEPS = 32700.0 / SPAN
LOW = TOP - SPAN
XMIN = 2.0 ** LOW


def log_code(x):
    size = jnp.log2(jnp.maximum(jnp.abs(x), XMIN)) * STEPS + (0.5 - LOW * STEPS)
    return jnp.where(x < 0, -size, size)


def log_value(code):
    size = jnp.exp2(jnp.abs(code) * (1.0 / STEPS) + LOW)
    return jnp.where(code == 0, 0.0, jnp.where(code < 0, -size, size))


def chain_code(x):
    x = x.reshape(32, 8, 256)
    top = jnp.max(jnp.abs(x), axis=0)
    power = jnp.ceil(jnp.log2(jnp.maximum(top, 1e-30)) * 64.0)
    q = x * (jnp.exp2(power * (-1.0 / 64.0)) * 32700.0)[None]
    q = jnp.where(q < 0, q - 0.5, q + 0.5)
    return q.reshape(256, 256).astype(I16), jnp.concatenate([power, power], axis=0).astype(I16)


def chain_value(codes, powers):
    scale = jnp.exp2(powers.astype(F32)[0:8] * (1.0 / 64.0)) * (1.0 / 32700.0)
    return (codes.astype(F32).reshape(32, 8, 256) * scale[None]).reshape(256, 256)


def kernel(amp_ref, int_hbm, map_ref, out_ref,
           g, b, f, e, r13, r04, d, sb, rb, fs, fr, pick,
           ag_send, ag_recv, sib_send, sib_recv, loc_sem,
           xa_send, xa_recv, xa_loc, rs_send, rs_recv, fin_send, fin_recv, fin_loc):
    i = lax.axis_index("ints")
    a = lax.axis_index("amp")
    zz, c = a // 2, lax.rem(a, 2)
    x, y = i // 4, lax.rem(i, 4)
    me = i * 2 + c
    zr, zl = lax.rem(zz + 1, 8), lax.rem(zz + 7, 8)
    right, left, sib = (i, zr * 2 + c), (i, zl * 2 + c), (i, zz * 2 + 1 - c)
    lane0 = pl.multiple_of(c * 64, 64)

    def peer(t):
        dj = t // 2
        j = lax.rem(x + dj // 4, 4) * 4 + lax.rem(y + lax.rem(dj, 4), 4)
        return j, lax.rem(c + lax.rem(t, 2), 2)

    load_b = pltpu.make_async_copy(int_hbm, b, loc_sem.at[0])
    load_b.start()
    own = pltpu.make_async_copy(amp_ref, g.at[0, pl.ds(lane0, 64)], loc_sem.at[1])
    own.start()

    barrier = pltpu.get_barrier_semaphore()

    def greet(t, carry):
        j, cc = peer(t)
        pl.semaphore_signal(barrier, inc=1, device_id=(j, zz * 2 + cc), device_id_type=MESH)
        return carry
    for zn in (zr, zl):
        for cc in (0, 1):
            pl.semaphore_signal(barrier, inc=1, device_id=(i, zn * 2 + cc), device_id_type=MESH)
    lax.fori_loop(1, 32, greet, 0)

    lane = lax.broadcasted_iota(jnp.int32, (128, 256), 0)
    ent = lax.broadcasted_iota(jnp.int32, (128, 256), 1)
    spread = (lane == zz * 16 + lax.rem(ent, 16)).astype(F32).astype(BF16)
    rows = jnp.dot(map_ref[...].astype(F32).astype(BF16), spread, preferred_element_type=F32)
    blk = lax.broadcasted_iota(jnp.int32, (16, 256), 0)
    ent16 = lax.broadcasted_iota(jnp.int32, (16, 256), 1)
    ids = jnp.sum(jnp.where(blk == ent16 // 16, rows, 0.0), axis=0, keepdims=True)
    tiles = lax.broadcasted_iota(jnp.int32, (256, 256), 0).astype(F32)
    pick[...] = jnp.where(tiles == ids, 1.0, 0.0).astype(BF16)

    pl.semaphore_wait(barrier, 35)

    def part(ref, p):
        return ref.at[pl.ds(pl.multiple_of(lane0 + p * 32, 32), 32)]

    def slot(direction, k):
        return 0 if k == 0 else 7 if k == 4 else 2 * k - 1 + direction

    def hop(direction, k, p):
        src = amp_ref.at[pl.ds(p * 32, 32)] if k == 1 else part(g.at[slot(direction, k - 1)], p)
        return pltpu.make_async_remote_copy(
            src_ref=src, dst_ref=part(g.at[slot(direction, k)], p),
            send_sem=ag_send.at[direction, k - 1, p], recv_sem=ag_recv.at[direction, k - 1, p],
            device_id=(right, left)[direction], device_id_type=MESH)

    def share(direction, k, p):
        ref = part(g.at[slot(direction, k)], p)
        return pltpu.make_async_remote_copy(
            src_ref=ref, dst_ref=ref,
            send_sem=sib_send.at[direction, k - 1, p], recv_sem=sib_recv.at[direction, k - 1, p],
            device_id=sib, device_id_type=MESH)

    def pieces(direction, k):
        return (0, 1) if k < 4 else (direction,)

    for p in (0, 1):
        for direction in (0, 1):
            hop(direction, 1, p).start()
    share0 = pltpu.make_async_remote_copy(
        src_ref=amp_ref, dst_ref=g.at[0, pl.ds(lane0, 64)], send_sem=loc_sem.at[2], recv_sem=loc_sem.at[3],
        device_id=sib, device_id_type=MESH)
    share0.start()

    def pass_on(k):
        for p in (0, 1):
            for direction in (0, 1):
                if p in pieces(direction, k):
                    hop(direction, k, p).wait_recv()
                    if k < 4 and p in pieces(direction, k + 1):
                        hop(direction, k + 1, p).start()
                    share(direction, k, p).start()
        for p in (0, 1):
            for direction in (0, 1):
                if p in pieces(direction, k):
                    share(direction, k, p).wait_recv()

    def multiply(first, count):
        m = count * 128

        def columns(n, carry):
            left_side = g[pl.ds(first, count)].reshape(m, 2048)
            acc = jnp.dot(left_side, b[:, pl.ds(pl.multiple_of(n * 256, 256), 256)], preferred_element_type=F32)
            code = log_code(acc)
            for s in (0, 1):
                f[pl.ds(2 * n + s, m, stride=8), :] = code[:, s * 128:(s + 1) * 128]
            return carry
        lax.fori_loop(0, 4, columns, 0)

        def pack(q, carry):
            base = pl.multiple_of(q * 256, 256)
            even = f[pl.ds(base, 128), :].reshape(16, 8, 128)
            odd = f[pl.ds(base + 128, 128), :].reshape(16, 8, 128)
            e[first + q // 4, lax.rem(q // 2, 2), lax.rem(q, 2)] = jnp.concatenate([even, odd], axis=1).astype(I16)
            return carry
        lax.fori_loop(0, 4 * count, pack, 0)

    def deal_refs(k, j, cc):
        if k in (0, 4):
            return e.at[0 if k == 0 else 7, cc, :, j], r04.at[k // 4, me]
        return e.at[2 * k - cc, :, :, j], r13.at[k - 1, me]

    def deal(k):
        def one(t, carry):
            j, cc = peer(t)
            src, dst = deal_refs(k, j, cc)
            pltpu.make_async_remote_copy(
                src_ref=src, dst_ref=dst, send_sem=xa_send.at[k], recv_sem=xa_recv.at[k],
                device_id=(j, zz * 2 + cc), device_id_type=MESH).start()
            return carry
        src, dst = deal_refs(k, i, c)
        pltpu.make_async_copy(src, dst, xa_loc.at[k]).start()
        lax.fori_loop(1, 32, one, 0)

    def deal_all(k):
        ref = (r04.at[k // 4] if k in (0, 4) else r13.at[k - 1]).at[pl.ds(0, 31)]
        return pltpu.make_async_remote_copy(
            src_ref=ref, dst_ref=ref, send_sem=xa_send.at[k], recv_sem=xa_recv.at[k],
            device_id=sib, device_id_type=MESH)

    def gathered(k):
        src, dst = deal_refs(k, i, c)
        pltpu.make_async_copy(src, dst, xa_loc.at[k]).wait()
        deal_all(k).wait_recv()

    def add_up(codes, at):
        v = log_value(codes.astype(F32)).reshape(32, 2, 8, 128)
        v = jnp.concatenate([v[:, 0].reshape(256, 128), v[:, 1].reshape(256, 128)], axis=1)
        hi = v.astype(BF16)
        lo = (v - hi.astype(F32)).astype(BF16)
        d[at] = (jnp.dot(pick[...], hi, preferred_element_type=F32)
                 + jnp.dot(pick[...], lo, preferred_element_type=F32))

    def dense(k):
        gathered(k)
        if k in (0, 4):
            def one(q, carry):
                add_up(r04[k // 4, :, q], (12 if k == 0 else 14) + q)
                return carry
            lax.fori_loop(0, 2, one, 0)
        else:
            def one(q, carry):
                add_up(r13[k - 1, :, q // 2, lax.rem(q, 2)], (k - 1) * 4 + q)
                return carry
            lax.fori_loop(0, 4, one, 0)

    ahead = jnp.where(c == 0, zr, zl)

    def chain(k, lane, p):
        m = p if k == 4 else (10, 6, 2)[k - 1] + lane * 2 + p
        to = m if k > 1 else 10 + c * 2 + p
        return m, pltpu.make_async_remote_copy(
            src_ref=sb.at[m], dst_ref=rb.at[to], send_sem=rs_send.at[m], recv_sem=rs_recv.at[to],
            device_id=(i, ahead * 2 + (c if k > 1 else lane)), device_id_type=MESH)

    def arrived(m):
        pltpu.make_async_remote_copy(
            src_ref=rb.at[m], dst_ref=rb.at[m], send_sem=rs_send.at[m], recv_sem=rs_recv.at[m],
            device_id=sib, device_id_type=MESH).wait_recv()
        return chain_value(rb[m, 0:256], rb[m, 256:272])

    def send_chain(k, lane, p):
        own_at = 14 + p if k == 4 else (k - 1) * 4 + lane * 2 + p
        value = d[own_at]
        if k < 3:
            value = value + arrived((6, 2)[k - 1] + lane * 2 + p)
        m, copy = chain(k, lane, p)
        sb[m, 0:256], sb[m, 256:272] = chain_code(value)
        copy.start()

    def send_chain3(p):
        value = d[8 + c * 2 + p] + arrived(p)
        m, copy = chain(3, c, p)
        sb[m, 0:256], sb[m, 256:272] = chain_code(value)
        copy.start()

    own.wait()
    share0.wait_recv()
    load_b.wait()
    multiply(0, 1)
    deal(0)
    for k in (1, 2, 3):
        pass_on(k)
        multiply(2 * k - 1, 2)
        deal(k)
        dense(k - 1)
    pass_on(4)
    multiply(7, 1)
    deal(4)
    dense(3)

    def rest3(p, carry):
        send_chain(3, 1 - c, p)
        return carry
    lax.fori_loop(0, 2, rest3, 0)
    dense(4)

    def first4(p, carry):
        send_chain(4, c, p)
        return carry
    lax.fori_loop(0, 2, first4, 0)

    def own3(p, carry):
        send_chain3(p)
        return carry
    lax.fori_loop(0, 2, own3, 0)
    for k in (2, 1):
        def step(q, carry):
            lane = jnp.where(q < 2, 1 - c, c)
            send_chain(k, lane, lax.rem(q, 2))
            return carry
        lax.fori_loop(0, 4, step, 0)

    def last(p, j):
        return pltpu.make_async_remote_copy(
            src_ref=fs.at[p, :, pl.ds(pl.multiple_of(j * 16, 16), 16)],
            dst_ref=fr.at[p, :, pl.ds(pl.multiple_of(i * 16, 16), 16)],
            send_sem=fin_send.at[p], recv_sem=fin_recv.at[p], device_id=(j, zz * 2 + c), device_id_type=MESH)

    def keep(p):
        mine = pl.ds(pl.multiple_of(i * 16, 16), 16)
        return pltpu.make_async_copy(fs.at[p, :, mine], fr.at[p, :, mine], fin_loc.at[p])

    for p in (0, 1):
        total = d[12 + p] + arrived(10 + p) + arrived(12 + p)
        fs[p, 0] = total[:, 0:128]
        fs[p, 1] = total[:, 128:256]
        keep(p).start()

        def owners(t, carry):
            j, _ = peer(2 * t)
            last(p, j).start()
            return carry
        lax.fori_loop(1, 16, owners, 0)
    for p in (0, 1):
        keep(p).wait()
        every = fr.at[p, :, pl.ds(0, 240)]
        done = pltpu.make_async_remote_copy(
            src_ref=every, dst_ref=every, send_sem=fin_send.at[p], recv_sem=fin_recv.at[p],
            device_id=sib, device_id_type=MESH)
        done.wait_recv()
        for rr in (0, 1):
            for t in range(16):
                out_ref[p * 32 + rr * 16:p * 32 + rr * 16 + 16, t * 128:(t + 1) * 128] = (
                    fr[p, rr, pl.ds(t, 16, stride=16), :])
        done.wait_send()

    share0.wait_send()
    for k in (1, 2, 3, 4):
        for direction in (0, 1):
            for p in pieces(direction, k):
                hop(direction, k, p).wait_send()
                share(direction, k, p).wait_send()
    for k in range(5):
        deal_all(k).wait_send()
    for m in range(14):
        pltpu.make_async_remote_copy(
            src_ref=sb.at[m], dst_ref=rb.at[m], send_sem=rs_send.at[m], recv_sem=rs_recv.at[m],
            device_id=sib, device_id_type=MESH).wait_send()


def local(amplitudes, integrals, tile_map, residual_in):
    dma = pltpu.SemaphoreType.DMA
    ladder = pl.pallas_call(
        kernel,
        name="ladder",
        out_shape=jax.ShapeDtypeStruct((64, 2048), F32),
        in_specs=[pl.BlockSpec(memory_space=pltpu.VMEM), pl.BlockSpec(memory_space=pl.ANY),
                  pl.BlockSpec(memory_space=pltpu.VMEM)],
        out_specs=pl.BlockSpec(memory_space=pltpu.VMEM),
        scratch_shapes=[
            pltpu.VMEM((8, 128, 2048), BF16),
            pltpu.VMEM((2048, 1024), BF16),
            pltpu.VMEM((2048, 128), F32),
            pltpu.VMEM((8, 2, 2, 16, 16, 128), I16),
            pltpu.VMEM((3, 32, 2, 2, 16, 128), I16),
            pltpu.VMEM((2, 32, 2, 16, 128), I16),
            pltpu.VMEM((16, 256, 256), F32),
            pltpu.VMEM((14, 272, 256), I16),
            pltpu.VMEM((14, 272, 256), I16),
            pltpu.VMEM((2, 2, 256, 128), F32),
            pltpu.VMEM((2, 2, 256, 128), F32),
            pltpu.VMEM((256, 256), BF16),
            dma((2, 4, 2)), dma((2, 4, 2)), dma((2, 4, 2)), dma((2, 4, 2)), dma((4,)),
            dma((5,)), dma((5,)), dma((5,)), dma((14,)), dma((14,)), dma((2,)), dma((2,)), dma((2,)),
        ],
        compiler_params=pltpu.CompilerParams(
            collective_id=0, has_side_effects=True, vmem_limit_bytes=56 * 2**20),
    )(amplitudes, integrals, tile_map)
    return residual_in + ladder


def solution(mesh):
    in_specs = (P("amp", "ints"), P("ints", "amp"), P(), P("amp", "ints"))
    out_specs = P("amp", "ints")
    return jax.shard_map(local, mesh=mesh, in_specs=in_specs, out_specs=out_specs, check_vma=False)
```

```python
import math

import jax
import jax.numpy as jnp
from jax import lax
from jax.experimental import pallas as pl
from jax.experimental.pallas import tpu as pltpu
from jax.sharding import PartitionSpec as P

MESH = pl.DeviceIdType.MESH
F32, BF16, I16 = jnp.float32, jnp.bfloat16, jnp.int16

TOP = math.log2(1537.0)
SPAN = 28.0
STEPS = 32700.0 / SPAN
LOW = TOP - SPAN
XMIN = 2.0 ** LOW


def log_code(x):
    size = jnp.log2(jnp.maximum(jnp.abs(x), XMIN)) * STEPS + (0.5 - LOW * STEPS)
    return jnp.where(x < 0, -size, size)


def log_value(code):
    size = jnp.exp2(jnp.abs(code) * (1.0 / STEPS) + LOW)
    return jnp.where(code == 0, 0.0, jnp.where(code < 0, -size, size))


def chain_code(x):
    x = x.reshape(32, 8, 256)
    top = jnp.max(jnp.abs(x), axis=0)
    power = jnp.ceil(jnp.log2(jnp.maximum(top, 1e-30)) * 64.0)
    q = x * (jnp.exp2(power * (-1.0 / 64.0)) * 32700.0)[None]
    q = jnp.where(q < 0, q - 0.5, q + 0.5)
    return q.reshape(256, 256).astype(I16), jnp.concatenate([power, power], axis=0).astype(I16)


def chain_value(codes, powers):
    scale = jnp.exp2(powers.astype(F32)[0:8] * (1.0 / 64.0)) * (1.0 / 32700.0)
    return (codes.astype(F32).reshape(32, 8, 256) * scale[None]).reshape(256, 256)


def kernel(amp_ref, int_hbm, map_ref, out_ref,
           g, b, f, e13, e04, r13, r04, d, sb, rb, fs, fr, pick,
           ag_send, ag_recv, sib_send, sib_recv, loc_sem,
           xa_send, xa_recv, xa_loc, rs_send, rs_recv, fin_send, fin_recv, fin_loc):
    i = lax.axis_index("ints")
    a = lax.axis_index("amp")
    zz, c = a // 2, lax.rem(a, 2)
    x, y = i // 4, lax.rem(i, 4)
    me = i * 2 + c
    zr, zl = lax.rem(zz + 1, 8), lax.rem(zz + 7, 8)
    right, left, sib = (i, zr * 2 + c), (i, zl * 2 + c), (i, zz * 2 + 1 - c)
    lane0 = pl.multiple_of(c * 64, 64)

    def peer(t):
        dj = t // 2
        j = lax.rem(x + dj // 4, 4) * 4 + lax.rem(y + lax.rem(dj, 4), 4)
        return j, lax.rem(c + lax.rem(t, 2), 2)

    barrier = pltpu.get_barrier_semaphore()

    def greet(t, carry):
        j, cc = peer(t)
        pl.semaphore_signal(barrier, inc=1, device_id=(j, zz * 2 + cc), device_id_type=MESH)
        return carry
    for zn in (zr, zl):
        for cc in (0, 1):
            pl.semaphore_signal(barrier, inc=1, device_id=(i, zn * 2 + cc), device_id_type=MESH)
    lax.fori_loop(1, 32, greet, 0)

    load_b = pltpu.make_async_copy(int_hbm, b, loc_sem.at[0])
    load_b.start()
    own = pltpu.make_async_copy(amp_ref, g.at[0, pl.ds(lane0, 64)], loc_sem.at[1])
    own.start()
    pl.semaphore_wait(barrier, 35)

    def part(ref, p):
        return ref.at[pl.ds(pl.multiple_of(lane0 + p * 32, 32), 32)]

    def slot(direction, k):
        return 0 if k == 0 else 7 if k == 4 else 2 * k - 1 + direction

    def hop(direction, k, p):
        src = amp_ref.at[pl.ds(p * 32, 32)] if k == 1 else part(g.at[slot(direction, k - 1)], p)
        return pltpu.make_async_remote_copy(
            src_ref=src, dst_ref=part(g.at[slot(direction, k)], p),
            send_sem=ag_send.at[direction, k - 1, p], recv_sem=ag_recv.at[direction, k - 1, p],
            device_id=(right, left)[direction], device_id_type=MESH)

    def share(direction, k, p):
        ref = part(g.at[slot(direction, k)], p)
        return pltpu.make_async_remote_copy(
            src_ref=ref, dst_ref=ref,
            send_sem=sib_send.at[direction, k - 1, p], recv_sem=sib_recv.at[direction, k - 1, p],
            device_id=sib, device_id_type=MESH)

    def pieces(direction, k):
        return (0, 1) if k < 4 else (direction,)

    for p in (0, 1):
        for direction in (0, 1):
            hop(direction, 1, p).start()
    share0 = pltpu.make_async_remote_copy(
        src_ref=amp_ref, dst_ref=g.at[0, pl.ds(lane0, 64)], send_sem=loc_sem.at[2], recv_sem=loc_sem.at[3],
        device_id=sib, device_id_type=MESH)
    share0.start()

    lane = lax.broadcasted_iota(jnp.int32, (128, 256), 0)
    ent = lax.broadcasted_iota(jnp.int32, (128, 256), 1)
    spread = (lane == zz * 16 + lax.rem(ent, 16)).astype(F32).astype(BF16)
    rows = jnp.dot(map_ref[...].astype(F32).astype(BF16), spread, preferred_element_type=F32)
    blk = lax.broadcasted_iota(jnp.int32, (16, 256), 0)
    ent16 = lax.broadcasted_iota(jnp.int32, (16, 256), 1)
    ids = jnp.sum(jnp.where(blk == ent16 // 16, rows, 0.0), axis=0, keepdims=True)
    tiles = lax.broadcasted_iota(jnp.int32, (256, 256), 0).astype(F32)
    pick[...] = jnp.where(tiles == ids, 1.0, 0.0).astype(BF16)

    def pass_on(k):
        for p in (0, 1):
            for direction in (0, 1):
                if p in pieces(direction, k):
                    hop(direction, k, p).wait_recv()
                    if k < 4 and p in pieces(direction, k + 1):
                        hop(direction, k + 1, p).start()
                    share(direction, k, p).start()

    def shared(k, halves=(0, 1)):
        for p in halves:
            for direction in (0, 1):
                if p in pieces(direction, k):
                    share(direction, k, p).wait_recv()

    def multiply(first, count):
        m = count * 128

        def columns(n, carry):
            left_side = g[pl.ds(first, count)].reshape(m, 2048)
            acc = jnp.dot(left_side, b[:, pl.ds(pl.multiple_of(n * 256, 256), 256)], preferred_element_type=F32)
            code = log_code(acc)
            for s in (0, 1):
                f[pl.ds(2 * n + s, m, stride=8), :] = code[:, s * 128:(s + 1) * 128]
            return carry
        lax.fori_loop(0, 4, columns, 0)

        def pack(q, carry):
            base = pl.multiple_of(q * 256, 256)
            even = f[pl.ds(base, 128), :].reshape(16, 8, 128)
            odd = f[pl.ds(base + 128, 128), :].reshape(16, 8, 128)
            codes = jnp.concatenate([even, odd], axis=1).astype(I16)
            blk_at, row_lane, rp = q // 4, lax.rem(q // 2, 2), lax.rem(q, 2)
            if count == 2:
                e13[first // 2, 1 - blk_at, :, row_lane, rp] = codes
            else:
                e04[first // 7, row_lane, :, rp] = codes
            return carry
        lax.fori_loop(0, 4 * count, pack, 0)

    def multiply3(p):
        def columns(n, carry):
            rows = jnp.concatenate([
                g[s, lane * 64 + p * 32:lane * 64 + p * 32 + 32] for s in (5, 6) for lane in (0, 1)], axis=0)
            acc = jnp.dot(rows, b[:, pl.ds(pl.multiple_of(n * 256, 256), 256)], preferred_element_type=F32)
            code = log_code(acc)
            for s in (0, 1):
                f[pl.ds(2 * n + s, 128, stride=8), :] = code[:, s * 128:(s + 1) * 128]
            return carry
        lax.fori_loop(0, 4, columns, 0)
        for q in range(4):
            even = f[q * 256:q * 256 + 128, :].reshape(16, 8, 128)
            odd = f[q * 256 + 128:q * 256 + 256, :].reshape(16, 8, 128)
            e13[2, 1 - q // 2, :, q % 2, p] = jnp.concatenate([even, odd], axis=1).astype(I16)

    def deal3(p):
        at = 3 if p == 0 else 5

        def refs(j, cc):
            return e13.at[2, cc, j, :, p], r13.at[2, me, :, p]
        src, dst = refs(i, c)
        pltpu.make_async_copy(src, dst, xa_loc.at[at]).start()

        def one(t, carry):
            j, cc = peer(t)
            src, dst = refs(j, cc)
            pltpu.make_async_remote_copy(
                src_ref=src, dst_ref=dst, send_sem=xa_send.at[at], recv_sem=xa_recv.at[at],
                device_id=(j, zz * 2 + cc), device_id_type=MESH).start()
            return carry
        lax.fori_loop(1, 32, one, 0)

    def deal3_all(p):
        at = 3 if p == 0 else 5
        ref = r13.at[2, pl.ds(0, 31), :, p]
        return pltpu.make_async_remote_copy(
            src_ref=ref, dst_ref=ref, send_sem=xa_send.at[at], recv_sem=xa_recv.at[at],
            device_id=sib, device_id_type=MESH)

    def gathered3(p):
        at = 3 if p == 0 else 5
        pltpu.make_async_copy(e13.at[2, c, i, :, p], r13.at[2, me, :, p], xa_loc.at[at]).wait()
        deal3_all(p).wait_recv()

    def deal_refs(k, j, cc):
        if k in (0, 4):
            return e04.at[k // 4, cc, j], r04.at[k // 4, me]
        return e13.at[k - 1, cc, j], r13.at[k - 1, me]

    def deal(k):
        def one(t, carry):
            j, cc = peer(t)
            src, dst = deal_refs(k, j, cc)
            pltpu.make_async_remote_copy(
                src_ref=src, dst_ref=dst, send_sem=xa_send.at[k], recv_sem=xa_recv.at[k],
                device_id=(j, zz * 2 + cc), device_id_type=MESH).start()
            return carry
        src, dst = deal_refs(k, i, c)
        pltpu.make_async_copy(src, dst, xa_loc.at[k]).start()
        lax.fori_loop(1, 32, one, 0)

    def deal_all(k):
        ref = (r04.at[k // 4] if k in (0, 4) else r13.at[k - 1]).at[pl.ds(0, 31)]
        return pltpu.make_async_remote_copy(
            src_ref=ref, dst_ref=ref, send_sem=xa_send.at[k], recv_sem=xa_recv.at[k],
            device_id=sib, device_id_type=MESH)

    def gathered(k):
        src, dst = deal_refs(k, i, c)
        pltpu.make_async_copy(src, dst, xa_loc.at[k]).wait()
        deal_all(k).wait_recv()

    def add_up(codes, at):
        v = log_value(codes.astype(F32)).reshape(32, 2, 8, 128)
        v = jnp.concatenate([v[:, 0].reshape(256, 128), v[:, 1].reshape(256, 128)], axis=1)
        hi = v.astype(BF16)
        lo = (v - hi.astype(F32)).astype(BF16)
        d[at] = (jnp.dot(pick[...], hi, preferred_element_type=F32)
                 + jnp.dot(pick[...], lo, preferred_element_type=F32))

    def dense(k):
        gathered(k)
        if k in (0, 4):
            def one(q, carry):
                add_up(r04[k // 4, :, q], (12 if k == 0 else 14) + q)
                return carry
            lax.fori_loop(0, 2, one, 0)
        else:
            def one(q, carry):
                add_up(r13[k - 1, :, q // 2, lax.rem(q, 2)], (k - 1) * 4 + q)
                return carry
            lax.fori_loop(0, 4, one, 0)

    ahead = jnp.where(c == 0, zr, zl)

    def chain(k, lane, p):
        m = p if k == 4 else (10, 6, 2)[k - 1] + lane * 2 + p
        to = m if k > 1 else 10 + c * 2 + p
        return m, pltpu.make_async_remote_copy(
            src_ref=sb.at[m], dst_ref=rb.at[to], send_sem=rs_send.at[m], recv_sem=rs_recv.at[to],
            device_id=(i, ahead * 2 + (c if k > 1 else lane)), device_id_type=MESH)

    def arrived(m):
        pltpu.make_async_remote_copy(
            src_ref=rb.at[m], dst_ref=rb.at[m], send_sem=rs_send.at[m], recv_sem=rs_recv.at[m],
            device_id=sib, device_id_type=MESH).wait_recv()
        return chain_value(rb[m, 0:256], rb[m, 256:272])

    def send_chain(k, lane, p):
        own_at = 14 + p if k == 4 else (k - 1) * 4 + lane * 2 + p
        value = d[own_at]
        if k < 3:
            value = value + arrived((6, 2)[k - 1] + lane * 2 + p)
        m, copy = chain(k, lane, p)
        sb[m, 0:256], sb[m, 256:272] = chain_code(value)
        copy.start()

    def send_chain3(p):
        value = d[8 + c * 2 + p] + arrived(p)
        m, copy = chain(3, c, p)
        sb[m, 0:256], sb[m, 256:272] = chain_code(value)
        copy.start()

    own.wait()
    share0.wait_recv()
    load_b.wait()
    multiply(0, 1)
    deal(0)
    pass_on(1)
    for k in (1, 2):
        shared(k)
        multiply(2 * k - 1, 2)
        pass_on(k + 1)
        deal(k)
        dense(k - 1)
    shared(3, (0,))
    multiply3(0)
    deal3(0)
    shared(3, (1,))
    multiply3(1)
    pass_on(4)
    deal3(1)
    shared(4)
    multiply(7, 1)
    deal(4)
    for p in (0, 1):
        gathered3(p)
        add_up(r13[2, :, 1 - c, p], 8 + (1 - c) * 2 + p)
        send_chain(3, 1 - c, p)
    for p in (0, 1):
        add_up(r13[2, :, c, p], 8 + c * 2 + p)
    dense(2)
    dense(4)

    def first4(p, carry):
        send_chain(4, c, p)
        return carry
    lax.fori_loop(0, 2, first4, 0)

    def run(k, lane):
        def one(p, carry):
            send_chain(k, lane, p)
            return carry
        lax.fori_loop(0, 2, one, 0)

    def own3(p, carry):
        send_chain3(p)
        return carry
    run(2, 1 - c)
    lax.fori_loop(0, 2, own3, 0)
    run(1, 1 - c)
    run(2, c)
    run(1, c)

    mine = pl.ds(pl.multiple_of(i * 32, 32), 32)

    def last(p, j):
        return pltpu.make_async_remote_copy(
            src_ref=fs.at[p, j].reshape(32, 128),
            dst_ref=fr.at[p, mine],
            send_sem=fin_send.at[p], recv_sem=fin_recv.at[p], device_id=(j, zz * 2 + c), device_id_type=MESH)

    def keep(p):
        return pltpu.make_async_copy(fs.at[p, i].reshape(32, 128), fr.at[p, mine], fin_loc.at[p])

    for p in (0, 1):
        total = d[12 + p] + arrived(10 + p) + arrived(12 + p)
        fs[p, :, 0] = total[:, 0:128].reshape(16, 16, 128)
        fs[p, :, 1] = total[:, 128:256].reshape(16, 16, 128)
        keep(p).start()

        def owners(t, carry):
            j, _ = peer(2 * t)
            last(p, j).start()
            return carry
        lax.fori_loop(1, 16, owners, 0)
    for p in (0, 1):
        keep(p).wait()
        every = fr.at[p, pl.ds(0, 480)]
        done = pltpu.make_async_remote_copy(
            src_ref=every, dst_ref=every, send_sem=fin_send.at[p], recv_sem=fin_recv.at[p],
            device_id=sib, device_id_type=MESH)
        done.wait_recv()
        for rr in (0, 1):
            for t in range(16):
                out_ref[p * 32 + rr * 16:p * 32 + rr * 16 + 16, t * 128:(t + 1) * 128] = (
                    fr[p, pl.ds(rr * 16 + t, 16, stride=32), :])
        done.wait_send()

    share0.wait_send()
    for k in (1, 2, 3, 4):
        for direction in (0, 1):
            for p in pieces(direction, k):
                hop(direction, k, p).wait_send()
                share(direction, k, p).wait_send()
    for k in (0, 1, 2, 4):
        deal_all(k).wait_send()
    deal3_all(0).wait_send()
    deal3_all(1).wait_send()
    for m in range(14):
        pltpu.make_async_remote_copy(
            src_ref=sb.at[m], dst_ref=rb.at[m], send_sem=rs_send.at[m], recv_sem=rs_recv.at[m],
            device_id=sib, device_id_type=MESH).wait_send()


def local(amplitudes, integrals, tile_map, residual_in):
    dma = pltpu.SemaphoreType.DMA
    ladder = pl.pallas_call(
        kernel,
        name="ladder",
        out_shape=jax.ShapeDtypeStruct((64, 2048), F32),
        in_specs=[pl.BlockSpec(memory_space=pl.ANY), pl.BlockSpec(memory_space=pl.ANY),
                  pl.BlockSpec(memory_space=pltpu.VMEM)],
        out_specs=pl.BlockSpec(memory_space=pltpu.VMEM),
        scratch_shapes=[
            pltpu.VMEM((8, 128, 2048), BF16),
            pltpu.VMEM((2048, 1024), BF16),
            pltpu.VMEM((2048, 128), F32),
            pltpu.VMEM((3, 2, 16, 2, 2, 16, 128), I16),
            pltpu.VMEM((2, 2, 16, 2, 16, 128), I16),
            pltpu.VMEM((3, 32, 2, 2, 16, 128), I16),
            pltpu.VMEM((2, 32, 2, 16, 128), I16),
            pltpu.VMEM((16, 256, 256), F32),
            pltpu.VMEM((14, 272, 256), I16),
            pltpu.VMEM((14, 272, 256), I16),
            pltpu.VMEM((2, 16, 2, 16, 128), F32),
            pltpu.VMEM((2, 512, 128), F32),
            pltpu.VMEM((256, 256), BF16),
            dma((2, 4, 2)), dma((2, 4, 2)), dma((2, 4, 2)), dma((2, 4, 2)), dma((4,)),
            dma((6,)), dma((6,)), dma((6,)), dma((14,)), dma((14,)), dma((2,)), dma((2,)), dma((2,)),
        ],
        compiler_params=pltpu.CompilerParams(
            collective_id=0, has_side_effects=True, vmem_limit_bytes=50 * 2**20),
    )(amplitudes, integrals, tile_map)
    return residual_in + ladder


def solution(mesh):
    in_specs = (P("amp", "ints"), P("ints", "amp"), P(), P("amp", "ints"))
    out_specs = P("amp", "ints")
    return jax.shard_map(local, mesh=mesh, in_specs=in_specs, out_specs=out_specs, check_vma=False)
```

```python
import math

import jax
import jax.numpy as jnp
from jax import lax
from jax.experimental import pallas as pl
from jax.experimental.pallas import tpu as pltpu
from jax.sharding import PartitionSpec as P

MESH = pl.DeviceIdType.MESH
F32, BF16, I16 = jnp.float32, jnp.bfloat16, jnp.int16

TOP = math.log2(1537.0)
SPAN = 28.0
STEPS = 32700.0 / SPAN
LOW = TOP - SPAN
XMIN = 2.0 ** LOW


def log_code(x):
    size = jnp.log2(jnp.maximum(jnp.abs(x), XMIN)) * STEPS + (0.5 - LOW * STEPS)
    return jnp.where(x < 0, -size, size)


def log_value(code):
    size = jnp.exp2(jnp.abs(code) * (1.0 / STEPS) + LOW)
    return jnp.where(code == 0, 0.0, jnp.where(code < 0, -size, size))


def chain_code(x):
    x = x.reshape(32, 8, 256)
    top = jnp.max(jnp.abs(x), axis=0)
    power = jnp.ceil(jnp.log2(jnp.maximum(top, 1e-30)) * 64.0)
    q = x * (jnp.exp2(power * (-1.0 / 64.0)) * 32700.0)[None]
    q = jnp.where(q < 0, q - 0.5, q + 0.5)
    q = q.reshape(256, 256).astype(I16)
    power = jnp.concatenate([power[:, 0:128], power[:, 128:256]], axis=0).astype(I16)
    return q[:, 0:128], q[:, 128:256], power


def chain_value(first, second, powers):
    scale = jnp.exp2(powers.astype(F32) * (1.0 / 64.0)) * (1.0 / 32700.0)
    first = first.astype(F32).reshape(32, 8, 128) * scale[None, 0:8]
    second = second.astype(F32).reshape(32, 8, 128) * scale[None, 8:16]
    return jnp.concatenate([first.reshape(256, 128), second.reshape(256, 128)], axis=1)


def final_code(total):
    x = total.reshape(16, 16, 256)
    top = jnp.max(jnp.abs(x), axis=1, keepdims=True)
    top = jnp.maximum(top[:, :, 0:128], top[:, :, 128:256])
    power = jnp.ceil(jnp.log2(jnp.maximum(top, 1e-30)) * 64.0)
    scale = jnp.exp2(power * (-1.0 / 64.0)) * 32700.0

    def whole(q):
        return jnp.where(q < 0, q - 0.5, q + 0.5).astype(I16)
    return (whole(x[:, :, 0:128] * scale), whole(x[:, :, 128:256] * scale),
            jnp.broadcast_to(power, (16, 16, 128)).astype(I16))


def kernel(amp_ref, int_hbm, map_ref, out_ref,
           g, b, f, e13, e04, r13, r04, d, sb, rb, fs, fr, pick,
           ag_send, ag_recv, sib_send, sib_recv, loc_sem,
           xa_send, xa_recv, xa_loc, rs_send, rs_recv, fin_send, fin_recv, fin_loc):
    i = lax.axis_index("ints")
    a = lax.axis_index("amp")
    zz, c = a // 2, lax.rem(a, 2)
    x, y = i // 4, lax.rem(i, 4)
    me = i * 2 + c
    zr, zl = lax.rem(zz + 1, 8), lax.rem(zz + 7, 8)
    right, left, sib = (i, zr * 2 + c), (i, zl * 2 + c), (i, zz * 2 + 1 - c)
    lane0 = pl.multiple_of(c * 64, 64)

    def peer(t):
        dj = t // 2
        j = lax.rem(x + dj // 4, 4) * 4 + lax.rem(y + lax.rem(dj, 4), 4)
        return j, lax.rem(c + lax.rem(t, 2), 2)

    barrier = pltpu.get_barrier_semaphore()

    def greet(t, carry):
        j, cc = peer(t)
        pl.semaphore_signal(barrier, inc=1, device_id=(j, zz * 2 + cc), device_id_type=MESH)
        return carry
    for zn in (zr, zl):
        for cc in (0, 1):
            pl.semaphore_signal(barrier, inc=1, device_id=(i, zn * 2 + cc), device_id_type=MESH)
    lax.fori_loop(1, 32, greet, 0)

    load_b = pltpu.make_async_copy(int_hbm, b, loc_sem.at[0])
    load_b.start()
    own = pltpu.make_async_copy(amp_ref, g.at[0, pl.ds(lane0, 64)], loc_sem.at[1])
    own.start()
    pl.semaphore_wait(barrier, 35)

    def part(ref, p):
        return ref.at[pl.ds(pl.multiple_of(lane0 + p * 32, 32), 32)]

    def slot(direction, k):
        return 0 if k == 0 else 7 if k == 4 else 2 * k - 1 + direction

    def hop(direction, k, p):
        src = amp_ref.at[pl.ds(p * 32, 32)] if k == 1 else part(g.at[slot(direction, k - 1)], p)
        return pltpu.make_async_remote_copy(
            src_ref=src, dst_ref=part(g.at[slot(direction, k)], p),
            send_sem=ag_send.at[direction, k - 1, p], recv_sem=ag_recv.at[direction, k - 1, p],
            device_id=(right, left)[direction], device_id_type=MESH)

    def share(direction, k, p):
        ref = part(g.at[slot(direction, k)], p)
        return pltpu.make_async_remote_copy(
            src_ref=ref, dst_ref=ref,
            send_sem=sib_send.at[direction, k - 1, p], recv_sem=sib_recv.at[direction, k - 1, p],
            device_id=sib, device_id_type=MESH)

    def pieces(direction, k):
        return (0, 1) if k < 4 else (direction,)

    for p in (0, 1):
        for direction in (0, 1):
            hop(direction, 1, p).start()
    share0 = pltpu.make_async_remote_copy(
        src_ref=amp_ref, dst_ref=g.at[0, pl.ds(lane0, 64)], send_sem=loc_sem.at[2], recv_sem=loc_sem.at[3],
        device_id=sib, device_id_type=MESH)
    share0.start()

    lane = lax.broadcasted_iota(jnp.int32, (128, 256), 0)
    ent = lax.broadcasted_iota(jnp.int32, (128, 256), 1)
    spread = (lane == zz * 16 + lax.rem(ent, 16)).astype(F32).astype(BF16)
    rows = jnp.dot(map_ref[...].astype(F32).astype(BF16), spread, preferred_element_type=F32)
    blk = lax.broadcasted_iota(jnp.int32, (16, 256), 0)
    ent16 = lax.broadcasted_iota(jnp.int32, (16, 256), 1)
    ids = jnp.sum(jnp.where(blk == ent16 // 16, rows, 0.0), axis=0, keepdims=True)
    tiles = lax.broadcasted_iota(jnp.int32, (256, 256), 0).astype(F32)
    pick[...] = jnp.where(tiles == ids, 1.0, 0.0).astype(BF16)

    def pass_on(k):
        for p in (0, 1):
            for direction in (0, 1):
                if p in pieces(direction, k):
                    hop(direction, k, p).wait_recv()
                    if k < 4 and p in pieces(direction, k + 1):
                        hop(direction, k + 1, p).start()
                    share(direction, k, p).start()

    def shared(k, halves=(0, 1)):
        for p in halves:
            for direction in (0, 1):
                if p in pieces(direction, k):
                    share(direction, k, p).wait_recv()

    def multiply(first, count):
        m = count * 128

        def columns(n, carry):
            left_side = g[pl.ds(first, count)].reshape(m, 2048)
            acc = jnp.dot(left_side, b[:, pl.ds(pl.multiple_of(n * 256, 256), 256)], preferred_element_type=F32)
            code = log_code(acc)
            for s in (0, 1):
                f[pl.ds(2 * n + s, m, stride=8), :] = code[:, s * 128:(s + 1) * 128]
            return carry
        lax.fori_loop(0, 4, columns, 0)

        def pack(q, carry):
            base = pl.multiple_of(q * 256, 256)
            even = f[pl.ds(base, 128), :].reshape(16, 8, 128)
            odd = f[pl.ds(base + 128, 128), :].reshape(16, 8, 128)
            codes = jnp.concatenate([even, odd], axis=1).astype(I16)
            blk_at, row_lane, rp = q // 4, lax.rem(q // 2, 2), lax.rem(q, 2)
            if count == 2:
                e13[first // 2, 1 - blk_at, :, row_lane, rp] = codes
            else:
                e04[first // 7, row_lane, :, rp] = codes
            return carry
        lax.fori_loop(0, 4 * count, pack, 0)

    def multiply3(p):
        def columns(n, carry):
            rows = jnp.concatenate([
                g[s, lane * 64 + p * 32:lane * 64 + p * 32 + 32] for s in (5, 6) for lane in (0, 1)], axis=0)
            acc = jnp.dot(rows, b[:, pl.ds(pl.multiple_of(n * 256, 256), 256)], preferred_element_type=F32)
            code = log_code(acc)
            for s in (0, 1):
                f[pl.ds(2 * n + s, 128, stride=8), :] = code[:, s * 128:(s + 1) * 128]
            return carry
        lax.fori_loop(0, 4, columns, 0)
        for q in range(4):
            even = f[q * 256:q * 256 + 128, :].reshape(16, 8, 128)
            odd = f[q * 256 + 128:q * 256 + 256, :].reshape(16, 8, 128)
            e13[2, 1 - q // 2, :, q % 2, p] = jnp.concatenate([even, odd], axis=1).astype(I16)

    def deal3(p):
        at = 3 if p == 0 else 5

        def refs(j, cc):
            return e13.at[2, cc, j, :, p], r13.at[2, me, :, p]
        src, dst = refs(i, c)
        pltpu.make_async_copy(src, dst, xa_loc.at[at]).start()

        def one(t, carry):
            j, cc = peer(t)
            src, dst = refs(j, cc)
            pltpu.make_async_remote_copy(
                src_ref=src, dst_ref=dst, send_sem=xa_send.at[at], recv_sem=xa_recv.at[at],
                device_id=(j, zz * 2 + cc), device_id_type=MESH).start()
            return carry
        lax.fori_loop(1, 32, one, 0)

    def deal3_all(p):
        at = 3 if p == 0 else 5
        ref = r13.at[2, pl.ds(0, 31), :, p]
        return pltpu.make_async_remote_copy(
            src_ref=ref, dst_ref=ref, send_sem=xa_send.at[at], recv_sem=xa_recv.at[at],
            device_id=sib, device_id_type=MESH)

    def gathered3(p):
        at = 3 if p == 0 else 5
        pltpu.make_async_copy(e13.at[2, c, i, :, p], r13.at[2, me, :, p], xa_loc.at[at]).wait()
        deal3_all(p).wait_recv()

    def deal_refs(k, j, cc):
        if k in (0, 4):
            return e04.at[k // 4, cc, j], r04.at[k // 4, me]
        return e13.at[k - 1, cc, j], r13.at[k - 1, me]

    def deal(k):
        def one(t, carry):
            j, cc = peer(t)
            src, dst = deal_refs(k, j, cc)
            pltpu.make_async_remote_copy(
                src_ref=src, dst_ref=dst, send_sem=xa_send.at[k], recv_sem=xa_recv.at[k],
                device_id=(j, zz * 2 + cc), device_id_type=MESH).start()
            return carry
        src, dst = deal_refs(k, i, c)
        pltpu.make_async_copy(src, dst, xa_loc.at[k]).start()
        lax.fori_loop(1, 32, one, 0)

    def deal_all(k):
        ref = (r04.at[k // 4] if k in (0, 4) else r13.at[k - 1]).at[pl.ds(0, 31)]
        return pltpu.make_async_remote_copy(
            src_ref=ref, dst_ref=ref, send_sem=xa_send.at[k], recv_sem=xa_recv.at[k],
            device_id=sib, device_id_type=MESH)

    def gathered(k):
        src, dst = deal_refs(k, i, c)
        pltpu.make_async_copy(src, dst, xa_loc.at[k]).wait()
        deal_all(k).wait_recv()

    def add_up(codes, at):
        v = log_value(codes.astype(F32)).reshape(32, 2, 8, 128)
        v = jnp.concatenate([v[:, 0].reshape(256, 128), v[:, 1].reshape(256, 128)], axis=1)
        hi = v.astype(BF16)
        lo = (v - hi.astype(F32)).astype(BF16)
        d[at] = (jnp.dot(pick[...], hi, preferred_element_type=F32)
                 + jnp.dot(pick[...], lo, preferred_element_type=F32))

    def dense(k):
        gathered(k)
        if k in (0, 4):
            def one(q, carry):
                add_up(r04[k // 4, :, q], (12 if k == 0 else 14) + q)
                return carry
            lax.fori_loop(0, 2, one, 0)
        else:
            def one(q, carry):
                add_up(r13[k - 1, :, q // 2, lax.rem(q, 2)], (k - 1) * 4 + q)
                return carry
            lax.fori_loop(0, 4, one, 0)

    ahead = jnp.where(c == 0, zr, zl)

    def chain(k, lane, p):
        m = p if k == 4 else (10, 6, 2)[k - 1] + lane * 2 + p
        to = m if k > 1 else 10 + c * 2 + p
        return m, pltpu.make_async_remote_copy(
            src_ref=sb.at[m], dst_ref=rb.at[to], send_sem=rs_send.at[m], recv_sem=rs_recv.at[to],
            device_id=(i, ahead * 2 + (c if k > 1 else lane)), device_id_type=MESH)

    def arrived(m):
        pltpu.make_async_remote_copy(
            src_ref=rb.at[m], dst_ref=rb.at[m], send_sem=rs_send.at[m], recv_sem=rs_recv.at[m],
            device_id=sib, device_id_type=MESH).wait_recv()
        return chain_value(rb[m, 0:256], rb[m, 256:512], rb[m, 512:528])

    def send_chain(k, lane, p):
        own_at = 14 + p if k == 4 else (k - 1) * 4 + lane * 2 + p
        value = d[own_at]
        if k < 3:
            value = value + arrived((6, 2)[k - 1] + lane * 2 + p)
        m, copy = chain(k, lane, p)
        sb[m, 0:256], sb[m, 256:512], sb[m, 512:528] = chain_code(value)
        copy.start()

    def send_chain3(p):
        value = d[8 + c * 2 + p] + arrived(p)
        m, copy = chain(3, c, p)
        sb[m, 0:256], sb[m, 256:512], sb[m, 512:528] = chain_code(value)
        copy.start()

    own.wait()
    share0.wait_recv()
    load_b.wait()
    multiply(0, 1)
    deal(0)
    pass_on(1)
    for k in (1, 2):
        shared(k)
        multiply(2 * k - 1, 2)
        pass_on(k + 1)
        deal(k)
        if k == 1:
            dense(0)
    shared(3, (0,))
    multiply3(0)
    deal3(0)
    shared(3, (1,))
    multiply3(1)
    pass_on(4)
    deal3(1)
    shared(4)
    multiply(7, 1)
    deal(4)
    for p in (0, 1):
        gathered3(p)
        add_up(r13[2, :, 1 - c, p], 8 + (1 - c) * 2 + p)
        send_chain(3, 1 - c, p)
    for p in (0, 1):
        add_up(r13[2, :, c, p], 8 + c * 2 + p)
    dense(4)

    def first4(p, carry):
        send_chain(4, c, p)
        return carry
    lax.fori_loop(0, 2, first4, 0)

    def run(k, lane):
        def one(p, carry):
            send_chain(k, lane, p)
            return carry
        lax.fori_loop(0, 2, one, 0)

    def own3(p, carry):
        send_chain3(p)
        return carry
    dense(2)
    dense(1)
    run(2, 1 - c)
    lax.fori_loop(0, 2, own3, 0)
    run(1, 1 - c)
    run(2, c)
    run(1, c)

    def last(p, j):
        return pltpu.make_async_remote_copy(
            src_ref=fs.at[p, j],
            dst_ref=fr.at[p, i],
            send_sem=fin_send.at[p], recv_sem=fin_recv.at[p], device_id=(j, zz * 2 + c), device_id_type=MESH)

    def keep(p):
        return pltpu.make_async_copy(fs.at[p, i], fr.at[p, i], fin_loc.at[p])

    for p in (0, 1):
        total = d[12 + p] + arrived(10 + p) + arrived(12 + p)
        fs[p, :, 0:16], fs[p, :, 16:32], fs[p, :, 32:48] = final_code(total)
        keep(p).start()

        def owners(t, carry):
            j, _ = peer(2 * t)
            last(p, j).start()
            return carry
        lax.fori_loop(1, 16, owners, 0)
    for p in (0, 1):
        keep(p).wait()
        every = fr.at[p, pl.ds(0, 15)]
        done = pltpu.make_async_remote_copy(
            src_ref=every, dst_ref=every, send_sem=fin_send.at[p], recv_sem=fin_recv.at[p],
            device_id=sib, device_id_type=MESH)
        done.wait_recv()
        scale = jnp.exp2(fr[p, :, 32:48].astype(F32) * (1.0 / 64.0)) * (1.0 / 32700.0)
        for rr in (0, 1):
            f[p * 512 + rr * 256:p * 512 + rr * 256 + 256, :] = (
                fr[p, :, rr * 16:rr * 16 + 16].astype(F32) * scale).reshape(256, 128)
            for t in range(16):
                out_ref[p * 32 + rr * 16:p * 32 + rr * 16 + 16, t * 128:(t + 1) * 128] = (
                    f[pl.ds(p * 512 + rr * 256 + t, 16, stride=16), :])
        done.wait_send()

    share0.wait_send()
    for k in (1, 2, 3, 4):
        for direction in (0, 1):
            for p in pieces(direction, k):
                hop(direction, k, p).wait_send()
                share(direction, k, p).wait_send()
    for k in (0, 1, 2, 4):
        deal_all(k).wait_send()
    deal3_all(0).wait_send()
    deal3_all(1).wait_send()
    for m in range(14):
        pltpu.make_async_remote_copy(
            src_ref=sb.at[m], dst_ref=rb.at[m], send_sem=rs_send.at[m], recv_sem=rs_recv.at[m],
            device_id=sib, device_id_type=MESH).wait_send()


def local(amplitudes, integrals, tile_map, residual_in):
    dma = pltpu.SemaphoreType.DMA
    ladder = pl.pallas_call(
        kernel,
        name="ladder",
        out_shape=jax.ShapeDtypeStruct((64, 2048), F32),
        in_specs=[pl.BlockSpec(memory_space=pl.ANY), pl.BlockSpec(memory_space=pl.ANY),
                  pl.BlockSpec(memory_space=pltpu.VMEM)],
        out_specs=pl.BlockSpec(memory_space=pltpu.VMEM),
        scratch_shapes=[
            pltpu.VMEM((8, 128, 2048), BF16),
            pltpu.VMEM((2048, 1024), BF16),
            pltpu.VMEM((2048, 128), F32),
            pltpu.VMEM((3, 2, 16, 2, 2, 16, 128), I16),
            pltpu.VMEM((2, 2, 16, 2, 16, 128), I16),
            pltpu.VMEM((3, 32, 2, 2, 16, 128), I16),
            pltpu.VMEM((2, 32, 2, 16, 128), I16),
            pltpu.VMEM((16, 256, 256), F32),
            pltpu.VMEM((14, 528, 128), I16),
            pltpu.VMEM((14, 528, 128), I16),
            pltpu.VMEM((2, 16, 48, 128), I16),
            pltpu.VMEM((2, 16, 48, 128), I16),
            pltpu.VMEM((256, 256), BF16),
            dma((2, 4, 2)), dma((2, 4, 2)), dma((2, 4, 2)), dma((2, 4, 2)), dma((4,)),
            dma((6,)), dma((6,)), dma((6,)), dma((14,)), dma((14,)), dma((2,)), dma((2,)), dma((2,)),
        ],
        compiler_params=pltpu.CompilerParams(
            collective_id=0, has_side_effects=True, vmem_limit_bytes=50 * 2**20),
    )(amplitudes, integrals, tile_map)
    return residual_in + ladder


def solution(mesh):
    in_specs = (P("amp", "ints"), P("ints", "amp"), P(), P("amp", "ints"))
    out_specs = P("amp", "ints")
    return jax.shard_map(local, mesh=mesh, in_specs=in_specs, out_specs=out_specs, check_vma=False)
```

```python
import math

import jax
import jax.numpy as jnp
from jax import lax
from jax.experimental import pallas as pl
from jax.experimental.pallas import tpu as pltpu
from jax.sharding import PartitionSpec as P

MESH = pl.DeviceIdType.MESH
F32, BF16, I16 = jnp.float32, jnp.bfloat16, jnp.int16

TOP = math.log2(1537.0)
SPAN = 28.0
STEPS = 32700.0 / SPAN
LOW = TOP - SPAN
XMIN = 2.0 ** LOW


def log_code(x):
    size = jnp.log2(jnp.maximum(jnp.abs(x), XMIN)) * STEPS + (0.5 - LOW * STEPS)
    return jnp.where(x < 0, -size, size)


def log_value(code):
    size = jnp.exp2(jnp.abs(code) * (1.0 / STEPS) + LOW)
    return jnp.where(code == 0, 0.0, jnp.where(code < 0, -size, size))


def chain_code(x):
    x = x.reshape(32, 8, 256)
    top = jnp.max(jnp.abs(x), axis=0)
    power = jnp.ceil(jnp.log2(jnp.maximum(top, 1e-30)) * 64.0)
    q = x * (jnp.exp2(power * (-1.0 / 64.0)) * 32700.0)[None]
    q = jnp.where(q < 0, q - 0.5, q + 0.5)
    q = q.reshape(256, 256).astype(I16)
    power = jnp.concatenate([power[:, 0:128], power[:, 128:256]], axis=0).astype(I16)
    return q[:, 0:128], q[:, 128:256], power


def chain_value(first, second, powers):
    scale = jnp.exp2(powers.astype(F32) * (1.0 / 64.0)) * (1.0 / 32700.0)
    first = first.astype(F32).reshape(32, 8, 128) * scale[None, 0:8]
    second = second.astype(F32).reshape(32, 8, 128) * scale[None, 8:16]
    return jnp.concatenate([first.reshape(256, 128), second.reshape(256, 128)], axis=1)


def final_code(total):
    x = total.reshape(16, 16, 256)
    top = jnp.max(jnp.abs(x), axis=1, keepdims=True)
    top = jnp.maximum(top[:, :, 0:128], top[:, :, 128:256])
    power = jnp.ceil(jnp.log2(jnp.maximum(top, 1e-30)) * 64.0)
    scale = jnp.exp2(power * (-1.0 / 64.0)) * 32700.0

    def whole(q):
        return jnp.where(q < 0, q - 0.5, q + 0.5).astype(I16)
    return (whole(x[:, :, 0:128] * scale), whole(x[:, :, 128:256] * scale),
            jnp.broadcast_to(power, (16, 16, 128)).astype(I16))


def kernel(amp_ref, int_hbm, map_ref, out_ref,
           g, b, f, e13, e04, r13, r04, d, sb, rb, fs, fr, pick,
           ag_send, ag_recv, sib_send, sib_recv, loc_sem,
           xa_send, xa_recv, xa_loc, rs_send, rs_recv, fin_send, fin_recv, fin_loc):
    i = lax.axis_index("ints")
    a = lax.axis_index("amp")
    zz, c = a // 2, lax.rem(a, 2)
    x, y = i // 4, lax.rem(i, 4)
    me = i * 2 + c
    zr, zl = lax.rem(zz + 1, 8), lax.rem(zz + 7, 8)
    right, left, sib = (i, zr * 2 + c), (i, zl * 2 + c), (i, zz * 2 + 1 - c)
    lane0 = pl.multiple_of(c * 64, 64)

    def peer(t):
        dj = t // 2
        j = lax.rem(x + dj // 4, 4) * 4 + lax.rem(y + lax.rem(dj, 4), 4)
        return j, lax.rem(c + lax.rem(t, 2), 2)

    barrier = pltpu.get_barrier_semaphore()

    def greet(t, carry):
        j, cc = peer(t)
        pl.semaphore_signal(barrier, inc=1, device_id=(j, zz * 2 + cc), device_id_type=MESH)
        return carry
    for zn in (zr, zl):
        for cc in (0, 1):
            pl.semaphore_signal(barrier, inc=1, device_id=(i, zn * 2 + cc), device_id_type=MESH)
    lax.fori_loop(1, 32, greet, 0)

    load_b = pltpu.make_async_copy(int_hbm, b, loc_sem.at[0])
    load_b.start()
    own = pltpu.make_async_copy(amp_ref, g.at[0, pl.ds(lane0, 64)], loc_sem.at[1])
    own.start()
    pl.semaphore_wait(barrier, 35)

    def part(ref, p):
        return ref.at[pl.ds(pl.multiple_of(lane0 + p * 32, 32), 32)]

    def slot(direction, k):
        return 0 if k == 0 else 7 if k == 4 else 2 * k - 1 + direction

    def hop(direction, k, p):
        src = amp_ref.at[pl.ds(p * 32, 32)] if k == 1 else part(g.at[slot(direction, k - 1)], p)
        return pltpu.make_async_remote_copy(
            src_ref=src, dst_ref=part(g.at[slot(direction, k)], p),
            send_sem=ag_send.at[direction, k - 1, p], recv_sem=ag_recv.at[direction, k - 1, p],
            device_id=(right, left)[direction], device_id_type=MESH)

    def share(direction, k, p):
        ref = part(g.at[slot(direction, k)], p)
        return pltpu.make_async_remote_copy(
            src_ref=ref, dst_ref=ref,
            send_sem=sib_send.at[direction, k - 1, p], recv_sem=sib_recv.at[direction, k - 1, p],
            device_id=sib, device_id_type=MESH)

    def pieces(direction, k):
        return (0, 1) if k < 4 else (direction,)

    for p in (0, 1):
        for direction in (0, 1):
            hop(direction, 1, p).start()
    share0 = pltpu.make_async_remote_copy(
        src_ref=amp_ref, dst_ref=g.at[0, pl.ds(lane0, 64)], send_sem=loc_sem.at[2], recv_sem=loc_sem.at[3],
        device_id=sib, device_id_type=MESH)
    share0.start()

    lane = lax.broadcasted_iota(jnp.int32, (128, 256), 0)
    ent = lax.broadcasted_iota(jnp.int32, (128, 256), 1)
    spread = (lane == zz * 16 + lax.rem(ent, 16)).astype(F32).astype(BF16)
    rows = jnp.dot(map_ref[...].astype(F32).astype(BF16), spread, preferred_element_type=F32)
    blk = lax.broadcasted_iota(jnp.int32, (16, 256), 0)
    ent16 = lax.broadcasted_iota(jnp.int32, (16, 256), 1)
    ids = jnp.sum(jnp.where(blk == ent16 // 16, rows, 0.0), axis=0, keepdims=True)
    tiles = lax.broadcasted_iota(jnp.int32, (256, 256), 0).astype(F32)
    pick[...] = jnp.where(tiles == ids, 1.0, 0.0).astype(BF16)

    def pass_on(k):
        for p in (0, 1):
            for direction in (0, 1):
                if p in pieces(direction, k):
                    hop(direction, k, p).wait_recv()
                    if k < 4 and p in pieces(direction, k + 1):
                        hop(direction, k + 1, p).start()
                    share(direction, k, p).start()

    def shared(k, halves=(0, 1)):
        for p in halves:
            for direction in (0, 1):
                if p in pieces(direction, k):
                    share(direction, k, p).wait_recv()

    def multiply(first, count):
        m = count * 128

        def columns(n, carry):
            left_side = g[pl.ds(first, count)].reshape(m, 2048)
            acc = jnp.dot(left_side, b[:, pl.ds(pl.multiple_of(n * 256, 256), 256)], preferred_element_type=F32)
            code = log_code(acc)
            for s in (0, 1):
                f[pl.ds(2 * n + s, m, stride=8), :] = code[:, s * 128:(s + 1) * 128]
            return carry
        lax.fori_loop(0, 4, columns, 0)

        def pack(q, carry):
            base = pl.multiple_of(q * 256, 256)
            even = f[pl.ds(base, 128), :].reshape(16, 8, 128)
            odd = f[pl.ds(base + 128, 128), :].reshape(16, 8, 128)
            codes = jnp.concatenate([even, odd], axis=1).astype(I16)
            blk_at, row_lane, rp = q // 4, lax.rem(q // 2, 2), lax.rem(q, 2)
            if count == 2:
                e13[first // 2, 1 - blk_at, :, row_lane, rp] = codes
            else:
                e04[first // 7, row_lane, :, rp] = codes
            return carry
        lax.fori_loop(0, 4 * count, pack, 0)

    def multiply3(p):
        def columns(n, carry):
            rows = jnp.concatenate([
                g[s, lane * 64 + p * 32:lane * 64 + p * 32 + 32] for s in (5, 6) for lane in (0, 1)], axis=0)
            acc = jnp.dot(rows, b[:, pl.ds(pl.multiple_of(n * 256, 256), 256)], preferred_element_type=F32)
            code = log_code(acc)
            for s in (0, 1):
                f[pl.ds(2 * n + s, 128, stride=8), :] = code[:, s * 128:(s + 1) * 128]
            return carry
        lax.fori_loop(0, 4, columns, 0)
        for q in range(4):
            even = f[q * 256:q * 256 + 128, :].reshape(16, 8, 128)
            odd = f[q * 256 + 128:q * 256 + 256, :].reshape(16, 8, 128)
            e13[2, 1 - q // 2, :, q % 2, p] = jnp.concatenate([even, odd], axis=1).astype(I16)

    def deal3(p):
        at = 3 if p == 0 else 5

        def refs(j, cc):
            return e13.at[2, cc, j, :, p], r13.at[2, me, :, p]
        src, dst = refs(i, c)
        pltpu.make_async_copy(src, dst, xa_loc.at[at]).start()

        def one(t, carry):
            j, cc = peer(t)
            src, dst = refs(j, cc)
            pltpu.make_async_remote_copy(
                src_ref=src, dst_ref=dst, send_sem=xa_send.at[at], recv_sem=xa_recv.at[at],
                device_id=(j, zz * 2 + cc), device_id_type=MESH).start()
            return carry
        lax.fori_loop(1, 32, one, 0)

    def deal3_all(p):
        at = 3 if p == 0 else 5
        ref = r13.at[2, pl.ds(0, 31), :, p]
        return pltpu.make_async_remote_copy(
            src_ref=ref, dst_ref=ref, send_sem=xa_send.at[at], recv_sem=xa_recv.at[at],
            device_id=sib, device_id_type=MESH)

    def gathered3(p):
        at = 3 if p == 0 else 5
        pltpu.make_async_copy(e13.at[2, c, i, :, p], r13.at[2, me, :, p], xa_loc.at[at]).wait()
        deal3_all(p).wait_recv()

    def deal_refs(k, j, cc):
        if k in (0, 4):
            return e04.at[k // 4, cc, j], r04.at[k // 4, me]
        return e13.at[k - 1, cc, j], r13.at[k - 1, me]

    def deal(k):
        def one(t, carry):
            j, cc = peer(t)
            src, dst = deal_refs(k, j, cc)
            pltpu.make_async_remote_copy(
                src_ref=src, dst_ref=dst, send_sem=xa_send.at[k], recv_sem=xa_recv.at[k],
                device_id=(j, zz * 2 + cc), device_id_type=MESH).start()
            return carry
        src, dst = deal_refs(k, i, c)
        pltpu.make_async_copy(src, dst, xa_loc.at[k]).start()
        lax.fori_loop(1, 32, one, 0)

    def deal_all(k):
        ref = (r04.at[k // 4] if k in (0, 4) else r13.at[k - 1]).at[pl.ds(0, 31)]
        return pltpu.make_async_remote_copy(
            src_ref=ref, dst_ref=ref, send_sem=xa_send.at[k], recv_sem=xa_recv.at[k],
            device_id=sib, device_id_type=MESH)

    def gathered(k):
        src, dst = deal_refs(k, i, c)
        pltpu.make_async_copy(src, dst, xa_loc.at[k]).wait()
        deal_all(k).wait_recv()

    def add_up(codes, at):
        v = log_value(codes.astype(F32)).reshape(32, 2, 8, 128)
        v = jnp.concatenate([v[:, 0].reshape(256, 128), v[:, 1].reshape(256, 128)], axis=1)
        hi = v.astype(BF16)
        lo = (v - hi.astype(F32)).astype(BF16)
        d[at] = (jnp.dot(pick[...], hi, preferred_element_type=F32)
                 + jnp.dot(pick[...], lo, preferred_element_type=F32))

    def dense(k):
        gathered(k)
        if k in (0, 4):
            def one(q, carry):
                add_up(r04[k // 4, :, q], (12 if k == 0 else 14) + q)
                return carry
            lax.fori_loop(0, 2, one, 0)
        else:
            def one(q, carry):
                add_up(r13[k - 1, :, q // 2, lax.rem(q, 2)], (k - 1) * 4 + q)
                return carry
            lax.fori_loop(0, 4, one, 0)

    ahead = jnp.where(c == 0, zr, zl)

    def chain(k, lane, p):
        m = p if k == 4 else (10, 6, 2)[k - 1] + lane * 2 + p
        to = m if k > 1 else 10 + c * 2 + p
        return m, pltpu.make_async_remote_copy(
            src_ref=sb.at[m], dst_ref=rb.at[to], send_sem=rs_send.at[m], recv_sem=rs_recv.at[to],
            device_id=(i, ahead * 2 + (c if k > 1 else lane)), device_id_type=MESH)

    def arrived(m):
        pltpu.make_async_remote_copy(
            src_ref=rb.at[m], dst_ref=rb.at[m], send_sem=rs_send.at[m], recv_sem=rs_recv.at[m],
            device_id=sib, device_id_type=MESH).wait_recv()
        return chain_value(rb[m, 0:256], rb[m, 256:512], rb[m, 512:528])

    def send_chain(k, lane, p):
        own_at = 14 + p if k == 4 else (k - 1) * 4 + lane * 2 + p
        value = d[own_at]
        if k < 3:
            value = value + arrived((6, 2)[k - 1] + lane * 2 + p)
        m, copy = chain(k, lane, p)
        sb[m, 0:256], sb[m, 256:512], sb[m, 512:528] = chain_code(value)
        copy.start()

    def send_chain3(p):
        value = d[8 + c * 2 + p] + arrived(p)
        m, copy = chain(3, c, p)
        sb[m, 0:256], sb[m, 256:512], sb[m, 512:528] = chain_code(value)
        copy.start()

    own.wait()
    share0.wait_recv()
    load_b.wait()
    multiply(0, 1)
    deal(0)
    pass_on(1)
    for k in (1, 2):
        shared(k)
        multiply(2 * k - 1, 2)
        pass_on(k + 1)
        deal(k)
        if k == 1:
            dense(0)
    shared(3, (0,))
    multiply3(0)
    deal3(0)
    shared(3, (1,))
    multiply3(1)
    pass_on(4)
    deal3(1)
    shared(4)
    multiply(7, 1)
    deal(4)
    for p in (0, 1):
        gathered3(p)
        add_up(r13[2, :, 1 - c, p], 8 + (1 - c) * 2 + p)
        send_chain(3, 1 - c, p)
    for p in (0, 1):
        add_up(r13[2, :, c, p], 8 + c * 2 + p)
    dense(4)

    def first4(p, carry):
        send_chain(4, c, p)
        return carry
    first4(0, 0)
    dense(2)
    first4(1, 0)

    def run(k, lane):
        def one(p, carry):
            send_chain(k, lane, p)
            return carry
        lax.fori_loop(0, 2, one, 0)

    def own3(p, carry):
        send_chain3(p)
        return carry
    dense(1)
    run(2, 1 - c)
    lax.fori_loop(0, 2, own3, 0)
    run(1, 1 - c)
    run(2, c)
    run(1, c)

    def last(p, j):
        return pltpu.make_async_remote_copy(
            src_ref=fs.at[p, j],
            dst_ref=fr.at[p, i],
            send_sem=fin_send.at[p], recv_sem=fin_recv.at[p], device_id=(j, zz * 2 + c), device_id_type=MESH)

    def keep(p):
        return pltpu.make_async_copy(fs.at[p, i], fr.at[p, i], fin_loc.at[p])

    for p in (0, 1):
        total = d[12 + p] + arrived(10 + p) + arrived(12 + p)
        fs[p, :, 0:16], fs[p, :, 16:32], fs[p, :, 32:48] = final_code(total)
        keep(p).start()

        def owners(t, carry):
            j, _ = peer(2 * t)
            last(p, j).start()
            return carry
        lax.fori_loop(1, 16, owners, 0)
    for p in (0, 1):
        keep(p).wait()
        every = fr.at[p, pl.ds(0, 15)]
        done = pltpu.make_async_remote_copy(
            src_ref=every, dst_ref=every, send_sem=fin_send.at[p], recv_sem=fin_recv.at[p],
            device_id=sib, device_id_type=MESH)
        done.wait_recv()
        scale = jnp.exp2(fr[p, :, 32:48].astype(F32) * (1.0 / 64.0)) * (1.0 / 32700.0)
        for rr in (0, 1):
            f[p * 512 + rr * 256:p * 512 + rr * 256 + 256, :] = (
                fr[p, :, rr * 16:rr * 16 + 16].astype(F32) * scale).reshape(256, 128)
            for t in range(16):
                out_ref[p * 32 + rr * 16:p * 32 + rr * 16 + 16, t * 128:(t + 1) * 128] = (
                    f[pl.ds(p * 512 + rr * 256 + t, 16, stride=16), :])
        done.wait_send()

    share0.wait_send()
    for k in (1, 2, 3, 4):
        for direction in (0, 1):
            for p in pieces(direction, k):
                hop(direction, k, p).wait_send()
                share(direction, k, p).wait_send()
    for k in (0, 1, 2, 4):
        deal_all(k).wait_send()
    deal3_all(0).wait_send()
    deal3_all(1).wait_send()
    for m in range(14):
        pltpu.make_async_remote_copy(
            src_ref=sb.at[m], dst_ref=rb.at[m], send_sem=rs_send.at[m], recv_sem=rs_recv.at[m],
            device_id=sib, device_id_type=MESH).wait_send()


def local(amplitudes, integrals, tile_map, residual_in):
    dma = pltpu.SemaphoreType.DMA
    ladder = pl.pallas_call(
        kernel,
        name="ladder",
        out_shape=jax.ShapeDtypeStruct((64, 2048), F32),
        in_specs=[pl.BlockSpec(memory_space=pl.ANY), pl.BlockSpec(memory_space=pl.ANY),
                  pl.BlockSpec(memory_space=pltpu.VMEM)],
        out_specs=pl.BlockSpec(memory_space=pltpu.VMEM),
        scratch_shapes=[
            pltpu.VMEM((8, 128, 2048), BF16),
            pltpu.VMEM((2048, 1024), BF16),
            pltpu.VMEM((2048, 128), F32),
            pltpu.VMEM((3, 2, 16, 2, 2, 16, 128), I16),
            pltpu.VMEM((2, 2, 16, 2, 16, 128), I16),
            pltpu.VMEM((3, 32, 2, 2, 16, 128), I16),
            pltpu.VMEM((2, 32, 2, 16, 128), I16),
            pltpu.VMEM((16, 256, 256), F32),
            pltpu.VMEM((14, 528, 128), I16),
            pltpu.VMEM((14, 528, 128), I16),
            pltpu.VMEM((2, 16, 48, 128), I16),
            pltpu.VMEM((2, 16, 48, 128), I16),
            pltpu.VMEM((256, 256), BF16),
            dma((2, 4, 2)), dma((2, 4, 2)), dma((2, 4, 2)), dma((2, 4, 2)), dma((4,)),
            dma((6,)), dma((6,)), dma((6,)), dma((14,)), dma((14,)), dma((2,)), dma((2,)), dma((2,)),
        ],
        compiler_params=pltpu.CompilerParams(
            collective_id=0, has_side_effects=True, vmem_limit_bytes=50 * 2**20),
    )(amplitudes, integrals, tile_map)
    return residual_in + ladder


def solution(mesh):
    in_specs = (P("amp", "ints"), P("ints", "amp"), P(), P("amp", "ints"))
    out_specs = P("amp", "ints")
    return jax.shard_map(local, mesh=mesh, in_specs=in_specs, out_specs=out_specs, check_vma=False)
```
